256 devices in a mesh: dp: 32 (over y_lo, z, core), tensor: 8 (over x, y_hi).
Axes of the slice: x: 4, y: 4 (y_hi: 2, y_lo: 2; y = y_hi * 2 + y_lo), z: 8, core: 2. Of those that a mesh axis runs over, the one named last changes fastest.
Arguments:
- tokens: bfloat16 [32768, 4096], P(('dp', 'tensor')), may hold values from -24 to 24
- out_grad: bfloat16 [32768, 2048], P('dp', 'tensor'), may hold values from -6 to 6
- weights: bfloat16 [4096, 2, 2048], P(None, None, 'tensor'), may hold values from -0.09375 to 0.09375
- master: float32 [4096, 2, 2048], P('dp', None, 'tensor'), may hold values from -0.09375 to 0.09375
- first_moment: float32 [4096, 2, 2048], P('dp', None, 'tensor'), may hold values from -4 to 4
- second_moment: float32 [4096, 2, 2048], P('dp', None, 'tensor'), may hold values from 0.05 to 5
Outputs:
- input_grad: bfloat16 [32768, 4096], P(('dp', 'tensor'))
- new_weights: bfloat16 [4096, 2, 2048], P(None, None, 'tensor')
- new_master: float32 [4096, 2, 2048], P('dp', None, 'tensor')
- new_first: float32 [4096, 2, 2048], P('dp', None, 'tensor')
- new_second: float32 [4096, 2, 2048], P('dp', None, 'tensor')
The draws below stay inside these ranges and needn't reach their ends.
All inputs are finite; a program needn't handle non-finite values.
Results may differ from the reference program's by a relative error of at most 0.012.
Values may be sent and summed in bfloat16 or wider, within the bound.
No kernel may reach another device: no remote copies, remote signals or barrier semaphores. Data moves between devices by JAX's collectives and lax.ppermute only.
A program may use at most 128 MiB of HBM per device.

```python
import math
import jax
import jax.numpy as jnp
from jax import lax

D = 4096
HID = 2048
SEQ = 512
BATCH = 2
TOKENS_ALL = 32768
N_DP = 32
N_TENSOR = 8


def raised(values, stream_key, source, target, shards_of, factor):
    owner, partner = [(jnp.arange(values.shape[axis_at]) // (values.shape[axis_at] // shards_of)).reshape([-1 if axis == axis_at else 1 for axis in range(values.ndim)]) for axis_at in (source, target)]
    chosen = jax.random.permutation(stream_key, shards_of)[partner]
    strong = (owner == chosen) | (owner == (partner + shards_of // 2) % shards_of)
    return jnp.where(strong, factor * values, values)


def block_levels(key, shape, cuts, least, largest):
    def one(position, blocks):
        steps = jax.random.uniform(jax.random.fold_in(jax.random.fold_in(key, 6), position), (blocks,), jnp.float32, least / len(cuts), largest / len(cuts))
        return jnp.repeat(jnp.exp(steps), shape[position] // blocks).reshape((-1,) + (1,) * (len(shape) - position - 1))

    gain = one(*cuts[0])
    for cut in cuts[1:]:
        gain = gain * one(*cut)
    return gain


def gaussian(stream_key, extent, scale, most, pieces=(), held_as=jnp.bfloat16):
    drawn = jax.random.normal(stream_key, extent, jnp.float32) * scale
    if len(pieces) > 0:
        drawn = block_levels(stream_key, extent, pieces, -0.22, 0.18) * drawn
    return jnp.clip(drawn, min=-most, max=most).astype(held_as)


def heavy_noise(rng, dims, scale, reach, pieces, heavy, held_as=jnp.bfloat16):
    drawn = scale * jax.random.normal(rng, dims, jnp.float32)
    if pieces:
        drawn = drawn * block_levels(rng, dims, pieces, -0.22, 0.18)
    return jnp.clip(raised(drawn, jax.random.fold_in(rng, 3), *heavy), -reach, reach).astype(held_as)


def setup_inputs(seed: int = 0) -> dict:
    streams_of = jax.random.split(jax.random.key(seed), 7)
    tokens = heavy_noise(streams_of[0], (TOKENS_ALL, D), 1.0, 24.0, ((0, 256),), (0, 1, 256, 6.0))
    out_grad = gaussian(streams_of[1], (TOKENS_ALL, HID), 1.0, 6.0, ((0, 32), (1, 8)))
    weights = gaussian(streams_of[2], (D, 2, HID), D ** -0.5, 0.09375, ((2, 8),))
    master = gaussian(streams_of[3], (D, 2, HID), D ** -0.5, 0.09375, ((0, 32), (2, 8)), jnp.float32)
    first_moment = gaussian(streams_of[4], (D, 2, HID), 0.5, 4.0, ((0, 32), (2, 8)), jnp.float32)
    second_moment = jnp.clip(jnp.exp(math.log(5.0) - 4.6051702 * jax.random.uniform(streams_of[5], (D, 2, HID), jnp.float32) ** block_levels(streams_of[5], (D, 2, HID), ((0, 32), (2, 8)), -0.2, 0.2)), 0.05, 5.0)
    return {"tokens": tokens, "out_grad": out_grad, "weights": weights, "master": master, "first_moment": first_moment, "second_moment": second_moment}


def linear_step(earlier, latter):
    return (earlier[0] * latter[0], latter[0] * earlier[1] + latter[1])

def local_backward(projected, out_grad):
    token_count = projected.shape[0]
    hidden_width = projected.shape[1] // 2
    shaped = (token_count // SEQ, SEQ, hidden_width)
    gate_value = jax.nn.sigmoid(projected[:, :hidden_width]).reshape(shaped)
    candidate = projected[:, hidden_width:].reshape(shaped)
    upstream = out_grad.astype(jnp.float32).reshape(shaped)
    retain = 1.0 - gate_value
    _, hidden_state = lax.associative_scan(linear_step, (retain, gate_value * candidate), axis=1)
    zeros_row = jnp.zeros_like(hidden_state[:, :1])
    previous = jnp.concatenate([zeros_row, hidden_state[:, :-1]], axis=1)
    retain_next = jnp.concatenate([retain[:, 1:], zeros_row], axis=1)
    _, flipped = lax.associative_scan(linear_step, (jnp.flip(retain_next, axis=1), jnp.flip(upstream, axis=1)), axis=1)
    adjoint = jnp.flip(flipped, axis=1)
    gate_grad = adjoint * (candidate - previous) * gate_value * retain
    candidate_grad = adjoint * gate_value
    joined = jnp.concatenate([gate_grad, candidate_grad], axis=2)
    return joined.reshape(token_count, 2 * hidden_width).astype(jnp.bfloat16)

def reference(tokens, out_grad, weights, master, first_moment, second_moment):
    token_count = BATCH * SEQ
    half_width = HID // N_TENSOR
    flat_weights = weights.reshape(D, 2 * HID)
    weight_parts = weights.reshape(D, 2, N_TENSOR, half_width)
    token_sets = tokens.reshape(N_DP, token_count, D)
    grad_sets = out_grad.reshape(N_DP, token_count, HID)

    def replica(running, element):
        inputs, upstream = element
        projected = jnp.dot(inputs, flat_weights, preferred_element_type=jnp.float32)
        pre_grad = local_backward(projected, upstream)
        grad_parts = pre_grad.reshape(token_count, 2, N_TENSOR, half_width)

        def shard_term(summed, shard_index):
            selected = lax.dynamic_index_in_dim(grad_parts, shard_index, 2, keepdims=False).reshape(token_count, 2 * half_width)
            columns = lax.dynamic_index_in_dim(weight_parts, shard_index, 2, keepdims=False).reshape(D, 2 * half_width)
            partial_value = lax.dot_general(selected, columns, (((1,), (1,)), ((), ())), preferred_element_type=jnp.float32)
            rounded = lax.optimization_barrier(partial_value.astype(jnp.bfloat16))
            return (summed + rounded.astype(jnp.float32), None)
        summed, _ = lax.scan(shard_term, jnp.zeros((token_count, D), jnp.float32), jnp.arange(N_TENSOR, dtype=jnp.int32))
        replica_grad = lax.dot_general(inputs, pre_grad, (((0,), (0,)), ((), ())), preferred_element_type=jnp.float32)
        return (running + replica_grad, summed.astype(jnp.bfloat16))
    gradient_sum, input_sets = lax.scan(replica, jnp.zeros((D, 2 * HID), jnp.float32), (token_sets, grad_sets))
    input_grad = input_sets.reshape(N_DP * token_count, D)
    gradient = gradient_sum.reshape(D, 2, HID) * (token_count * N_DP) ** (-0.5)
    new_first = 0.9 * first_moment + 0.1 * gradient
    new_second = 0.95 * second_moment + 0.05 * gradient * gradient
    update = new_first / (1.0 - 0.9 ** 10) / (jnp.sqrt(new_second / (1.0 - 0.95 ** 10)) + 1e-08)
    new_master = master - 0.001 * (update + 0.1 * master)
    return (input_grad, new_master.astype(jnp.bfloat16), new_master, new_first, new_second)
```

```python
import jax, jax.numpy as jnp
from jax import lax
from jax.experimental import pallas as pl
from jax.experimental.pallas import tpu as pltpu
from jax.sharding import PartitionSpec as P

SEQ = 512
GROUP = 8

def scan_kernel(projected_ref, upstream_ref, out_ref, gate_ref, slope_ref):
    width = upstream_ref.shape[1]
    sequences = upstream_ref.shape[0] // SEQ
    row = lax.broadcasted_iota(jnp.int32, (GROUP, width), 0)
    zero = jnp.zeros((GROUP, width), jnp.float32)

    def down(x, k, fill):
        return jnp.where(row >= k, pltpu.roll(x, k, axis=0), fill)

    def up(x, k, fill):
        return jnp.where(row < GROUP - k, pltpu.roll(x, GROUP - k, axis=0), fill)

    def forward(step, carries):
        after = []
        for sequence in range(sequences):
            carry = carries[sequence]
            for half in range(2):
                rows = pl.ds(pl.multiple_of(sequence * SEQ + step * 16, 16) + half * 8, GROUP)
                gate = jax.nn.sigmoid(projected_ref[rows, :width])
                candidate = projected_ref[rows, width:]
                retain = 1.0 - gate
                factor, total = retain, gate * candidate
                for k in (1, 2, 4):
                    total = total + factor * down(total, k, 0.0)
                    factor = factor * down(factor, k, 1.0)
                hidden = total + factor * carry
                previous = jnp.where(row >= 1, pltpu.roll(hidden, 1, axis=0), carry)
                carry = jnp.broadcast_to(hidden[GROUP - 1 :], (GROUP, width))
                gate_ref[rows, :] = gate
                slope_ref[rows, :] = (candidate - previous) * gate * retain
            after.append(carry)
        return tuple(after)

    lax.fori_loop(0, SEQ // 16, forward, (zero,) * sequences, unroll=2)

    def backward(index, carries):
        step = SEQ // 16 - 1 - index
        after = []
        for sequence in range(sequences):
            carry = carries[sequence]
            base = pl.multiple_of(sequence * SEQ + step * 16, 16)
            upstream = upstream_ref[pl.ds(base, 16), :].astype(jnp.float32)
            halves = [None, None]
            for half in (1, 0):
                rows = pl.ds(base + half * 8, GROUP)
                incoming = upstream[half * 8 : half * 8 + 8]
                gate = gate_ref[rows, :]
                retain = 1.0 - gate
                factor, total = retain, retain * incoming
                for k in (1, 2, 4):
                    total = total + factor * up(total, k, 0.0)
                    factor = factor * up(factor, k, 1.0)
                passed = total + factor * carry
                adjoint = incoming + jnp.where(
                    row < GROUP - 1, pltpu.roll(passed, GROUP - 1, axis=0), carry
                )
                carry = jnp.broadcast_to(passed[:1], (GROUP, width))
                halves[half] = (adjoint * slope_ref[rows, :], adjoint * gate)
            after.append(carry)
            out_ref[pl.ds(base, 16), :width] = jnp.concatenate(
                [halves[0][0], halves[1][0]], axis=0
            ).astype(jnp.bfloat16)
            out_ref[pl.ds(base, 16), width:] = jnp.concatenate(
                [halves[0][1], halves[1][1]], axis=0
            ).astype(jnp.bfloat16)
        return tuple(after)

    lax.fori_loop(0, SEQ // 16, backward, (zero,) * sequences, unroll=2)


def local_backward(projected, upstream):
    token_count, width = upstream.shape
    return pl.pallas_call(
        scan_kernel,
        out_shape=jax.ShapeDtypeStruct((token_count, 2 * width), jnp.bfloat16),
        in_specs=[pl.BlockSpec(memory_space=pltpu.VMEM)] * 2,
        out_specs=pl.BlockSpec(memory_space=pltpu.VMEM),
        scratch_shapes=[
            pltpu.VMEM((token_count, width), jnp.float32),
            pltpu.VMEM((token_count, width), jnp.float32),
        ],
        compiler_params=pltpu.CompilerParams(vmem_limit_bytes=16 * 1024 * 1024),
        cost_estimate=pl.CostEstimate(
            flops=60 * token_count * width, bytes_accessed=14 * token_count * width,
            transcendentals=token_count * width,
        ),
    )(projected, upstream)


def adamw_update(gradient, master, first_moment, second_moment):
    new_first = 0.9 * first_moment + 0.1 * gradient
    new_second = 0.95 * second_moment + 0.05 * gradient * gradient
    update = new_first / (1.0 - 0.9**10) / (jnp.sqrt(new_second / (1.0 - 0.95**10)) + 1e-08)
    new_master = master - 0.001 * (update + 0.1 * master)
    return (new_master, new_first, new_second)


def body(tokens, out_grad, weights, master, first_moment, second_moment):
    model_width = weights.shape[0]
    half_width = weights.shape[2]
    flat_weights = weights.reshape(model_width, 2 * half_width)
    gathered = lax.all_gather(tokens, "tensor", axis=0, tiled=True)
    projected = jnp.dot(gathered, flat_weights, preferred_element_type=jnp.float32)
    pre_grad = local_backward(projected, out_grad)
    replicas = lax.axis_size("dp")
    owner_rows = model_width // replicas
    loss_scale = (gathered.shape[0] * replicas) ** (-0.5)
    product = lax.dot_general(
        gathered, pre_grad, (((0,), (0,)), ((), ())), preferred_element_type=jnp.float32
    )
    gradient_sum = lax.psum_scatter(
        product.astype(jnp.bfloat16), "dp", scatter_dimension=0, tiled=True
    )
    gradient_sum = gradient_sum.reshape(owner_rows, 2, half_width).astype(jnp.float32)
    input_sum = lax.psum_scatter(
        lax.dot_general(
            pre_grad, flat_weights, (((1,), (1,)), ((), ())), preferred_element_type=jnp.float32
        ).astype(jnp.bfloat16),
        "tensor",
        scatter_dimension=0,
        tiled=True,
    )
    new_master, new_first, new_second = adamw_update(
        gradient_sum * loss_scale, master, first_moment, second_moment
    )
    new_weights = lax.all_gather(new_master.astype(jnp.bfloat16), "dp", axis=0, tiled=True)
    return (input_sum, new_weights, new_master, new_first, new_second)


def solution(mesh):
    return jax.shard_map(
        body,
        mesh=mesh,
        in_specs=(
            P(("dp", "tensor"), None),
            P("dp", "tensor"),
            P(None, None, "tensor"),
            P("dp", None, "tensor"),
            P("dp", None, "tensor"),
            P("dp", None, "tensor"),
        ),
        out_specs=(
            P(("dp", "tensor"), None),
            P(None, None, "tensor"),
            P("dp", None, "tensor"),
            P("dp", None, "tensor"),
            P("dp", None, "tensor"),
        ),
        check_vma=False,
    )
```

```python
import jax, jax.numpy as jnp
from jax import lax
from jax.experimental import pallas as pl
from jax.experimental.pallas import tpu as pltpu
from jax.sharding import Mesh, PartitionSpec as P

SEQ = 512
GROUP = 8

def scan_kernel(projected_ref, upstream_ref, out_ref, gate_ref, slope_ref):
    width = upstream_ref.shape[1]
    sequences = upstream_ref.shape[0] // SEQ
    row = lax.broadcasted_iota(jnp.int32, (GROUP, width), 0)
    zero = jnp.zeros((GROUP, width), jnp.float32)

    def down(x, k, fill):
        return jnp.where(row >= k, pltpu.roll(x, k, axis=0), fill)

    def up(x, k, fill):
        return jnp.where(row < GROUP - k, pltpu.roll(x, GROUP - k, axis=0), fill)

    def forward(step, carries):
        after = []
        for sequence in range(sequences):
            carry = carries[sequence]
            for half in range(2):
                rows = pl.ds(pl.multiple_of(sequence * SEQ + step * 16, 16) + half * 8, GROUP)
                gate = jax.nn.sigmoid(projected_ref[rows, :width])
                candidate = projected_ref[rows, width:]
                retain = 1.0 - gate
                factor, total = retain, gate * candidate
                for k in (1, 2, 4):
                    total = total + factor * down(total, k, 0.0)
                    factor = factor * down(factor, k, 1.0)
                hidden = total + factor * carry
                previous = jnp.where(row >= 1, pltpu.roll(hidden, 1, axis=0), carry)
                carry = jnp.broadcast_to(hidden[GROUP - 1 :], (GROUP, width))
                gate_ref[rows, :] = gate
                slope_ref[rows, :] = (candidate - previous) * gate * retain
            after.append(carry)
        return tuple(after)

    lax.fori_loop(0, SEQ // 16, forward, (zero,) * sequences, unroll=2)

    def backward(index, carries):
        step = SEQ // 16 - 1 - index
        after = []
        for sequence in range(sequences):
            carry = carries[sequence]
            base = pl.multiple_of(sequence * SEQ + step * 16, 16)
            upstream = upstream_ref[pl.ds(base, 16), :].astype(jnp.float32)
            halves = [None, None]
            for half in (1, 0):
                rows = pl.ds(base + half * 8, GROUP)
                incoming = upstream[half * 8 : half * 8 + 8]
                gate = gate_ref[rows, :]
                retain = 1.0 - gate
                factor, total = retain, retain * incoming
                for k in (1, 2, 4):
                    total = total + factor * up(total, k, 0.0)
                    factor = factor * up(factor, k, 1.0)
                passed = total + factor * carry
                adjoint = incoming + jnp.where(
                    row < GROUP - 1, pltpu.roll(passed, GROUP - 1, axis=0), carry
                )
                carry = jnp.broadcast_to(passed[:1], (GROUP, width))
                halves[half] = (adjoint * slope_ref[rows, :], adjoint * gate)
            after.append(carry)
            out_ref[pl.ds(base, 16), :width] = jnp.concatenate(
                [halves[0][0], halves[1][0]], axis=0
            ).astype(jnp.bfloat16)
            out_ref[pl.ds(base, 16), width:] = jnp.concatenate(
                [halves[0][1], halves[1][1]], axis=0
            ).astype(jnp.bfloat16)
        return tuple(after)

    lax.fori_loop(0, SEQ // 16, backward, (zero,) * sequences, unroll=2)


def local_backward(projected, upstream):
    token_count, width = upstream.shape
    return pl.pallas_call(
        scan_kernel,
        out_shape=jax.ShapeDtypeStruct((token_count, 2 * width), jnp.bfloat16),
        in_specs=[pl.BlockSpec(memory_space=pltpu.VMEM)] * 2,
        out_specs=pl.BlockSpec(memory_space=pltpu.VMEM),
        scratch_shapes=[
            pltpu.VMEM((token_count, width), jnp.float32),
            pltpu.VMEM((token_count, width), jnp.float32),
        ],
        compiler_params=pltpu.CompilerParams(vmem_limit_bytes=16 * 1024 * 1024),
        cost_estimate=pl.CostEstimate(
            flops=60 * token_count * width, bytes_accessed=14 * token_count * width,
            transcendentals=token_count * width,
        ),
    )(projected, upstream)


def adamw_update(gradient, master, first_moment, second_moment):
    new_first = 0.9 * first_moment + 0.1 * gradient
    new_second = 0.95 * second_moment + 0.05 * gradient * gradient
    update = new_first / (1.0 - 0.9**10) / (jnp.sqrt(new_second / (1.0 - 0.95**10)) + 1e-08)
    new_master = master - 0.001 * (update + 0.1 * master)
    return (new_master, new_first, new_second)


def shift(values, axis, step):
    size = lax.axis_size(axis)
    return lax.ppermute(values, axis, [(i, (i + step) % size) for i in range(size)])


def together(*values):
    return lax.optimization_barrier(values)


def gather_tokens(tokens):
    rows, width = tokens.shape
    half = rows // 2
    at_x, at_y = lax.axis_index("x"), lax.axis_index("y_hi")
    cut = width // 2
    first, second = tokens[:, :cut], tokens[:, cut:]
    gathered = jnp.zeros((8 * rows, width), tokens.dtype)

    def put(gathered, block, dx, dy, row, column):
        owner = lax.rem(at_x + dx, 4) * 2 + lax.rem(at_y + dy, 2)
        return lax.dynamic_update_slice(gathered, block, (owner * rows + row, column))

    first_left, first_right = shift(first, "x", 1), shift(first, "x", 3)
    second_swap = shift(second, "y_hi", 1)
    first_swap = shift(first, "y_hi", 1)
    first_left, first_right, second_swap = together(first_left, first_right, second_swap)

    pair = jnp.concatenate([second, second_swap], axis=0)
    sides = jnp.concatenate([first_left, first_right], axis=0)
    far_top, far_bottom = shift(first_left[:half], "x", 1), shift(first_right[half:], "x", 3)
    pair_left, pair_right = shift(pair, "x", 1), shift(pair, "x", 3)
    sides_swap = shift(sides, "y_hi", 1)
    far_top, far_bottom, pair_left, pair_right = together(
        far_top, far_bottom, pair_left, pair_right
    )

    far = jnp.concatenate([far_top, far_bottom], axis=0)
    far_swap = shift(far, "y_hi", 1)
    pair_far_own, pair_far_other = shift(pair_left[:rows], "x", 1), shift(pair_right[rows:], "x", 3)

    gathered = put(gathered, tokens, 0, 0, 0, 0)
    gathered = put(gathered, first_left, 3, 0, 0, 0)
    gathered = put(gathered, first_right, 1, 0, 0, 0)
    gathered = put(gathered, second_swap, 0, 1, 0, cut)
    gathered = put(gathered, first_swap, 0, 1, 0, 0)
    gathered = put(gathered, far, 2, 0, 0, 0)
    for block, dx in ((pair_left, 3), (pair_right, 1)):
        gathered = put(gathered, block[:rows], dx, 0, 0, cut)
        gathered = put(gathered, block[rows:], dx, 1, 0, cut)
    gathered = put(gathered, sides_swap[:rows], 3, 1, 0, 0)
    gathered = put(gathered, sides_swap[rows:], 1, 1, 0, 0)
    gathered = put(gathered, far_swap, 2, 1, 0, 0)
    gathered = put(gathered, pair_far_own, 2, 0, 0, cut)
    gathered = put(gathered, pair_far_other, 2, 1, 0, cut)
    return gathered


def sum_on_owners(pre_grad, gathered):
    at_core, at_z, at_y = (lax.axis_index(name) for name in ("core", "z", "y_lo"))
    width = pre_grad.shape[1] // 2
    depth = gathered.shape[1]
    chips = 16
    rows = depth // chips

    def half_product(core):
        selected = lax.dynamic_slice_in_dim(pre_grad, core * width, width, axis=1)
        return lax.dot_general(
            selected, gathered, (((0,), (0,)), ((), ())), preferred_element_type=jnp.float32
        ).astype(jnp.bfloat16)

    sent = shift(half_product(1 - at_core), "core", 1)
    kept = half_product(at_core)
    summed = (kept.astype(jnp.float32) + sent.astype(jnp.float32)).astype(jnp.bfloat16)
    summed = summed.reshape(width, 2, 8, rows)

    def chunk(distance):
        return lax.dynamic_slice_in_dim(
            summed, lax.rem(at_z + distance, 8), 1, axis=2
        ).reshape(width, 2 * rows)

    def add(*values):
        total = values[0].astype(jnp.float32)
        for value in values[1:]:
            total = total + value.astype(jnp.float32)
        return total.astype(jnp.bfloat16)

    up, down = chunk(4), chunk(5)
    for step in range(4):
        up = shift(up, "z", 1)
        if step < 3:
            down = shift(down, "z", 7)
            up, down = together(up, down)
            up = add(up, chunk(3 - step))
            if step < 2:
                down = add(down, chunk(6 + step))
    total = add(chunk(0), up, down).reshape(width, 2, rows)
    own = lax.dynamic_slice_in_dim(total, at_y, 1, axis=1).reshape(width, rows)
    other = lax.dynamic_slice_in_dim(total, 1 - at_y, 1, axis=1).reshape(width, rows)
    total = add(own, shift(other, "y_lo", 1)).reshape(width, 2, rows // 2)
    own = lax.dynamic_slice_in_dim(total, at_core, 1, axis=1).reshape(width, rows // 2)
    other = lax.dynamic_slice_in_dim(total, 1 - at_core, 1, axis=1).reshape(width, rows // 2)
    other = shift(other, "core", 1)
    gate = jnp.where(at_core == 0, own, other)
    candidate = jnp.where(at_core == 0, other, own)
    return jnp.stack([gate.T, candidate.T], axis=1).astype(jnp.float32)


def gather_weights(owned):
    at_core, at_z, at_y = (lax.axis_index(name) for name in ("core", "z", "y_lo"))
    result = jnp.zeros((2, 8, 2) + owned.shape, owned.dtype)
    swapped = shift(owned, "y_lo", 1)
    low = jnp.where(at_y == 0, owned, swapped)
    high = jnp.where(at_y == 0, swapped, owned)
    pair = jnp.stack([low, high], axis=0)

    def put(result, block, distance, core):
        return lax.dynamic_update_slice(
            result, block[:, None, None], (0, lax.rem(at_z + distance, 8), core, 0, 0, 0)
        )

    def put_both(result, parts):
        distances = [distance for distance, _ in parts]
        crossed = shift(jnp.stack([block for _, block in parts]), "core", 1)
        for position, (distance, block) in enumerate(parts):
            result = put(result, block, distance, at_core)
            result = put(result, crossed[position], distance, 1 - at_core)
        return result

    parts = [(0, pair)]
    up, down = pair, pair
    for step in range(4):
        up = shift(up, "z", 1)
        if step < 3:
            down = shift(down, "z", 7)
            up, down = together(up, down)
            parts.append((1 + step, down))
        parts.append((7 - step, up))
        if step == 1:
            result = put_both(result, parts[:5])
    result = put_both(result, parts[5:])
    return result.reshape((32 * owned.shape[0],) + owned.shape[1:])


def body(tokens, out_grad, weights, master, first_moment, second_moment):
    model_width = weights.shape[0]
    half_width = weights.shape[2]
    flat_weights = weights.reshape(model_width, 2 * half_width)
    gathered = gather_tokens(tokens)
    projected = jnp.dot(gathered, flat_weights, preferred_element_type=jnp.float32)
    pre_grad = local_backward(projected, out_grad)
    loss_scale = (gathered.shape[0] * 32) ** (-0.5)
    input_sum = lax.psum_scatter(
        lax.dot_general(
            pre_grad, flat_weights, (((1,), (1,)), ((), ())), preferred_element_type=jnp.float32
        ).astype(jnp.bfloat16),
        ("x", "y_hi"),
        scatter_dimension=0,
        tiled=True,
    )
    gradient_sum = sum_on_owners(pre_grad, gathered)
    new_master, new_first, new_second = adamw_update(
        gradient_sum * loss_scale, master, first_moment, second_moment
    )
    new_weights = gather_weights(new_master.astype(jnp.bfloat16))
    return (input_sum, new_weights, new_master, new_first, new_second)


def solution(mesh):
    dp, tensor = ("y_lo", "z", "core"), ("x", "y_hi")
    split = Mesh(mesh.devices.reshape(2, 8, 2, 4, 2), dp + tensor)
    owners = P(dp, None, tensor)
    return jax.shard_map(
        body,
        mesh=split,
        in_specs=(
            P(dp + tensor, None),
            P(dp, tensor),
            P(None, None, tensor),
            owners,
            owners,
            owners,
        ),
        out_specs=(P(dp + tensor, None), P(None, None, tensor), owners, owners, owners),
        check_vma=False,
    )
```

```python
import jax, jax.numpy as jnp
from jax import lax
from jax.experimental import pallas as pl
from jax.experimental.layout import Layout, with_layout_constraint
from jax.experimental.pallas import tpu as pltpu
from jax.sharding import Mesh, PartitionSpec as P

SEQ = 512
GROUP = 8

def scan_kernel(projected_ref, upstream_ref, out_ref, turned_ref, gate_ref, slope_ref):
    width = upstream_ref.shape[1]
    sequences = upstream_ref.shape[0] // SEQ
    row = lax.broadcasted_iota(jnp.int32, (GROUP, width), 0)
    zero = jnp.zeros((GROUP, width), jnp.float32)

    def down(x, k, fill):
        return jnp.where(row >= k, pltpu.roll(x, k, axis=0), fill)

    def up(x, k, fill):
        return jnp.where(row < GROUP - k, pltpu.roll(x, GROUP - k, axis=0), fill)

    def forward(step, carries):
        after = []
        for sequence in range(sequences):
            carry = carries[sequence]
            for half in range(2):
                rows = pl.ds(pl.multiple_of(sequence * SEQ + step * 16, 16) + half * 8, GROUP)
                gate = jax.nn.sigmoid(projected_ref[rows, :width])
                candidate = projected_ref[rows, width:]
                retain = 1.0 - gate
                factor, total = retain, gate * candidate
                for k in (1, 2, 4):
                    total = total + factor * down(total, k, 0.0)
                    factor = factor * down(factor, k, 1.0)
                hidden = total + factor * carry
                previous = jnp.where(row >= 1, pltpu.roll(hidden, 1, axis=0), carry)
                carry = jnp.broadcast_to(hidden[GROUP - 1 :], (GROUP, width))
                gate_ref[rows, :] = gate
                slope_ref[rows, :] = (candidate - previous) * gate * retain
            after.append(carry)
        return tuple(after)

    lax.fori_loop(0, SEQ // 16, forward, (zero,) * sequences, unroll=2)

    def backward(index, carries):
        step = SEQ // 16 - 1 - index
        after = []
        for sequence in range(sequences):
            carry = carries[sequence]
            base = pl.multiple_of(sequence * SEQ + step * 16, 16)
            upstream = upstream_ref[pl.ds(base, 16), :].astype(jnp.float32)
            halves = [None, None]
            for half in (1, 0):
                rows = pl.ds(base + half * 8, GROUP)
                incoming = upstream[half * 8 : half * 8 + 8]
                gate = gate_ref[rows, :]
                retain = 1.0 - gate
                factor, total = retain, retain * incoming
                for k in (1, 2, 4):
                    total = total + factor * up(total, k, 0.0)
                    factor = factor * up(factor, k, 1.0)
                passed = total + factor * carry
                adjoint = incoming + jnp.where(
                    row < GROUP - 1, pltpu.roll(passed, GROUP - 1, axis=0), carry
                )
                carry = jnp.broadcast_to(passed[:1], (GROUP, width))
                halves[half] = (adjoint * slope_ref[rows, :], adjoint * gate)
            after.append(carry)
            out_ref[pl.ds(base, 16), :width] = jnp.concatenate(
                [halves[0][0], halves[1][0]], axis=0
            ).astype(jnp.bfloat16)
            out_ref[pl.ds(base, 16), width:] = jnp.concatenate(
                [halves[0][1], halves[1][1]], axis=0
            ).astype(jnp.bfloat16)
        return tuple(after)

    lax.fori_loop(0, SEQ // 16, backward, (zero,) * sequences, unroll=2)
    turned_ref[...] = out_ref[...].T


def local_backward(projected, upstream):
    token_count, width = upstream.shape
    return pl.pallas_call(
        scan_kernel,
        out_shape=[
            jax.ShapeDtypeStruct((token_count, 2 * width), jnp.bfloat16),
            jax.ShapeDtypeStruct((2 * width, token_count), jnp.bfloat16),
        ],
        in_specs=[pl.BlockSpec(memory_space=pltpu.VMEM)] * 2,
        out_specs=[pl.BlockSpec(memory_space=pltpu.VMEM)] * 2,
        scratch_shapes=[
            pltpu.VMEM((token_count, width), jnp.float32),
            pltpu.VMEM((token_count, width), jnp.float32),
        ],
        compiler_params=pltpu.CompilerParams(vmem_limit_bytes=16 * 1024 * 1024),
        cost_estimate=pl.CostEstimate(
            flops=60 * token_count * width, bytes_accessed=14 * token_count * width,
            transcendentals=token_count * width,
        ),
    )(projected, upstream)


def adamw_update(gradient, master, first_moment, second_moment):
    new_first = 0.9 * first_moment + 0.1 * gradient
    new_second = 0.95 * second_moment + 0.05 * gradient * gradient
    update = new_first / (1.0 - 0.9**10) / (jnp.sqrt(new_second / (1.0 - 0.95**10)) + 1e-08)
    new_master = master - 0.001 * (update + 0.1 * master)
    return (new_master, new_first, new_second)


def shift(values, axis, step):
    size = lax.axis_size(axis)
    return lax.ppermute(values, axis, [(i, (i + step) % size) for i in range(size)])


def together(*values):
    return lax.optimization_barrier(values)


def gather_tokens(tokens, weights):
    rows, width = tokens.shape
    half = rows // 2
    at_x, at_y = lax.axis_index("x"), lax.axis_index("y_hi")
    cut = width // 2
    first, second = tokens[:, :cut], tokens[:, cut:]
    gathered = jnp.zeros((8 * rows, width), tokens.dtype)

    def put(gathered, block, dx, dy, row, column):
        owner = lax.rem(at_x + dx, 4) * 2 + lax.rem(at_y + dy, 2)
        return lax.dynamic_update_slice(gathered, block, (owner * rows + row, column))

    first_left, first_right = shift(first, "x", 1), shift(first, "x", 3)
    second_swap = shift(second, "y_hi", 1)
    (late,) = after(weights, first)
    first_swap = shift(late, "y_hi", 1)
    first_left, first_right, second_swap = together(first_left, first_right, second_swap)

    pair = jnp.concatenate([second, second_swap], axis=0)
    sides = jnp.concatenate([first_left, first_right], axis=0)
    far_top, far_bottom = shift(first_left[:half], "x", 1), shift(first_right[half:], "x", 3)
    pair_left, pair_right = shift(pair, "x", 1), shift(pair, "x", 3)
    sides_swap = shift(sides, "y_hi", 1)
    far_top, far_bottom, pair_left, pair_right = together(
        far_top, far_bottom, pair_left, pair_right
    )

    far = jnp.concatenate([far_top, far_bottom], axis=0)
    far_swap = shift(far, "y_hi", 1)
    pair_far_own, pair_far_other = shift(pair_left[:rows], "x", 1), shift(pair_right[rows:], "x", 3)

    gathered = put(gathered, tokens, 0, 0, 0, 0)
    gathered = put(gathered, first_left, 3, 0, 0, 0)
    gathered = put(gathered, first_right, 1, 0, 0, 0)
    gathered = put(gathered, second_swap, 0, 1, 0, cut)
    gathered = put(gathered, first_swap, 0, 1, 0, 0)
    gathered = put(gathered, far, 2, 0, 0, 0)
    for block, dx in ((pair_left, 3), (pair_right, 1)):
        gathered = put(gathered, block[:rows], dx, 0, 0, cut)
        gathered = put(gathered, block[rows:], dx, 1, 0, cut)
    gathered = put(gathered, sides_swap[:rows], 3, 1, 0, 0)
    gathered = put(gathered, sides_swap[rows:], 1, 1, 0, 0)
    gathered = put(gathered, far_swap, 2, 1, 0, 0)
    gathered = put(gathered, pair_far_own, 2, 0, 0, cut)
    gathered = put(gathered, pair_far_other, 2, 1, 0, cut)
    return gathered


def around(values):
    up = [(2 * i, 2 * ((i + 1) % 8)) for i in range(8)]
    down = [(2 * i + 1, 2 * ((i + 7) % 8) + 1) for i in range(8)]
    return lax.ppermute(values, ("z", "core"), up + down)


def add(*values):
    total = values[0].astype(jnp.float32)
    for value in values[1:]:
        total = total + value.astype(jnp.float32)
    return total.astype(jnp.bfloat16)


def products_kernel(order_ref, turned_ref, tokens_ref, out_ref):
    out_ref[0] = jnp.dot(
        turned_ref[...], tokens_ref[...], preferred_element_type=jnp.float32
    ).astype(out_ref.dtype)


def products(turned, gathered, order):
    width, token_count = turned.shape
    rows = gathered.shape[1] // 16
    steps = len(order)
    return pl.pallas_call(
        products_kernel,
        out_shape=jax.ShapeDtypeStruct((steps, width, rows), jnp.bfloat16),
        grid_spec=pltpu.PrefetchScalarGridSpec(
            num_scalar_prefetch=1,
            grid=(steps,),
            in_specs=[
                pl.BlockSpec((width, token_count), lambda step, order: (0, 0)),
                pl.BlockSpec((token_count, rows), lambda step, order: (0, order[step])),
            ],
            out_specs=pl.BlockSpec((1, width, rows), lambda step, order: (step, 0, 0)),
        ),
        compiler_params=pltpu.CompilerParams(vmem_limit_bytes=8 * 1024 * 1024),
        cost_estimate=pl.CostEstimate(
            flops=2 * steps * width * rows * token_count,
            bytes_accessed=2 * (token_count * (width + steps * rows) + steps * width * rows),
            transcendentals=0,
        ),
    )(jnp.stack(order).astype(jnp.int32), turned, gathered)


def after(token, *values):
    return together(token, *values)[1:]


def sum_on_owners(pre_grad, turned, gathered, terms):
    at_core, at_z, at_y = (lax.axis_index(name) for name in ("core", "z", "y_lo"))
    sign = 1 - 2 * at_core
    rows = gathered.shape[1] // 16
    rings = [1 - at_y, at_y]

    def place(distance, y):
        return y * 8 + lax.rem(at_z + distance + 8, 8)

    def columns(total):
        own = lax.dynamic_slice_in_dim(total, at_core * (rows // 2), rows // 2, axis=1)
        other = lax.dynamic_slice_in_dim(total, (1 - at_core) * (rows // 2), rows // 2, axis=1)
        return own, other

    far = products(turned, gathered, [place(4, 1 - at_core), place(4, at_core)])
    crossed_far = shift(far[0], "core", 1)
    (late,) = after(far, pre_grad)
    offloaded = terms.start(late)
    (far, crossed_far) = after(offloaded, far, crossed_far)
    far = add(far[1], crossed_far)
    (late,) = after(far, turned)
    far = around(far)
    sent, kept = [], []
    for distance in (3, 2, 1):
        sent += [place(-sign * distance, y) for y in rings]
        kept += [place(sign * distance, y) for y in rings]
    kept += [place(0, y) for y in rings]
    sent = products(late, gathered, sent)
    crossed = shift(sent, "core", 1)
    (late,) = after(sent, turned)
    kept = products(late, gathered, kept)
    none = jnp.zeros((), far.dtype)
    running = [jnp.where(y == at_core, far, none) for y in rings]
    for step in range(3):
        for ring in range(2):
            position = 2 * step + ring
            near = kept[position]
            if step == 2 and ring == 0:
                near = together(near, *terms.second())[0]
            value = add(near, crossed[position], running[ring])
            running[ring] = around(value)
        if step == 0:
            terms.first(value)
    straight, diagonal = columns(add(kept[6], running[0]))
    straight = shift(straight, "y_lo", 1)
    diagonal = lax.ppermute(diagonal, ("y_lo", "core"), [(i, 3 - i) for i in range(4)])
    own, crossed = columns(add(kept[7], running[1]))
    crossed = shift(crossed, "core", 1)
    total = sum(value.astype(jnp.float32) for value in (own, crossed, straight, diagonal))
    return total.T.reshape(rows // 2, 2, -1)


def row_major(values):
    return with_layout_constraint(values, Layout(major_to_minor=tuple(range(values.ndim))))


def place_kernel(block_ref, out_ref, semaphore):
    at_y, at_z = lax.axis_index("y_lo"), lax.axis_index("z")
    copy = pltpu.make_async_copy(block_ref, out_ref.at[at_y, at_z], semaphore)
    copy.start()
    copy.wait()


def place(block):
    return pl.pallas_call(
        place_kernel,
        out_shape=jax.ShapeDtypeStruct((2, 8) + block.shape, block.dtype),
        in_specs=[pl.BlockSpec(memory_space=pltpu.VMEM)],
        out_specs=pl.BlockSpec(memory_space=pl.ANY),
        scratch_shapes=[pltpu.SemaphoreType.DMA],
        cost_estimate=pl.CostEstimate(flops=0, bytes_accessed=4 * block.size, transcendentals=0),
    )(block)


def gather_weights(owned, terms):
    at_core, at_z, at_y = (lax.axis_index(name) for name in ("core", "z", "y_lo"))
    sign = 1 - 2 * at_core
    rows = owned.shape[0]
    rings = [at_y, 1 - at_y]

    def put(result, block, distance, y, row=0):
        return lax.dynamic_update_slice(
            result, block[None, None], (y, lax.rem(at_z + distance + 8, 8), row, 0, 0)
        )

    def swap(values, axis):
        return row_major(shift(values, axis, 1))

    def by_core(mine, others):
        return row_major(
            jnp.where(
                at_core == 0,
                jnp.concatenate([mine, others], axis=0),
                jnp.concatenate([others, mine], axis=0),
            )
        )

    owned = row_major(owned)
    across = swap(owned, "y_lo")
    moving = [by_core(owned, swap(owned, "core"))]
    received = [row_major(around(moving[0]))]
    (across,) = after(moving[0], across)
    moving.append(by_core(across, swap(across, "core")))
    received.append(row_major(around(moving[1])))
    terms.third(moving[1])
    result = put(place(moving[0]), moving[1], 0, rings[1])
    for step in (1, 2, 3):
        for ring, y in enumerate(rings):
            moving = received[ring]
            if step < 3:
                received[ring] = row_major(around(moving))
            else:
                sent = lax.dynamic_slice_in_dim(moving, at_core * rows, rows, axis=0)
                received[ring] = row_major(around(row_major(sent)))
            crossed = swap(moving, "core")
            result = put(result, moving, -sign * step, y)
            result = put(result, crossed, sign * step, y)
            result, received[ring] = together(result, received[ring])
    terms.last(received[0])
    for ring, y in enumerate(rings):
        crossed = swap(received[ring], "core")
        result = put(result, received[ring], 4, y, at_core * rows)
        result = put(result, crossed, 4, y, (1 - at_core) * rows)
    return result.reshape((32 * rows,) + owned.shape[1:])


def terms_kernel(pre_ref, weights_ref, out_ref):
    out_ref[...] = lax.dot_general(
        pre_ref[...],
        weights_ref[...],
        (((1,), (1,)), ((), ())),
        preferred_element_type=jnp.float32,
    ).astype(out_ref.dtype)


def all_terms(pre_grad, weights, columns):
    token_count, width = pre_grad.shape
    block = 512
    return pl.pallas_call(
        terms_kernel,
        out_shape=jax.ShapeDtypeStruct((token_count, columns), pre_grad.dtype),
        grid=(columns // block,),
        in_specs=[
            pl.BlockSpec((token_count, width), lambda step: (0, 0)),
            pl.BlockSpec((block, width), lambda step: (step, 0)),
        ],
        out_specs=pl.BlockSpec((token_count, block), lambda step: (0, step)),
        compiler_params=pltpu.CompilerParams(vmem_limit_bytes=12 * 1024 * 1024),
        cost_estimate=pl.CostEstimate(
            flops=2 * token_count * width * columns,
            bytes_accessed=2 * (token_count * width + columns * (width + token_count)),
            transcendentals=0,
        ),
    )(pre_grad, weights)


class Terms:
    def __init__(self, weights, offloaded):
        self.weights = weights
        self.offloaded = offloaded

    def dot(self, values, weights):
        return lax.dot_general(
            values, weights, (((1,), (1,)), ((), ())), preferred_element_type=jnp.float32
        ).astype(jnp.bfloat16)

    def part(self, distance):
        rows = self.pre_grad.shape[0] // 4
        start = lax.rem(lax.axis_index("x") + distance, 4) * rows
        values = lax.dynamic_slice_in_dim(self.pre_grad, start, rows, axis=0)
        return self.dot(values, self.weights[self.offloaded :])

    def start(self, pre_grad):
        self.pre_grad = pre_grad
        self.rows = pre_grad.shape[0] // 8
        offloaded = all_terms(pre_grad, self.weights, self.offloaded)
        self.sum = lax.psum_scatter(offloaded, ("x", "y_hi"), scatter_dimension=0, tiled=True)
        return offloaded

    def first(self, token):
        (self.pre_grad,) = after(token, self.pre_grad)
        far = self.part(2)
        self.moved = shift(far[: self.rows], "x", 1), shift(far[self.rows :], "x", 3)
        return far

    def second(self):
        from_left, from_right = self.moved
        rows = self.rows
        right, left = self.part(1), self.part(3)
        right = jnp.concatenate([add(right[:rows], from_left), right[rows:]], axis=0)
        left = jnp.concatenate([left[:rows], add(left[rows:], from_right)], axis=0)
        self.moved = shift(right, "x", 1), shift(left, "x", 3)
        return right, left

    def third(self, token):
        from_left, from_right = after(token, *self.moved)
        at_y = lax.axis_index("y_hi")
        total = add(self.part(0), from_left, from_right).reshape(2, self.rows, -1)
        self.own = lax.dynamic_index_in_dim(total, at_y, 0, keepdims=False)
        other = lax.dynamic_index_in_dim(total, 1 - at_y, 0, keepdims=False)
        self.moved = shift(other, "y_hi", 1)

    def last(self, token):
        (moved,) = after(token, self.moved)
        self.rest = add(self.own, moved)


def body(tokens, out_grad, weights, master, first_moment, second_moment):
    model_width = weights.shape[0]
    half_width = weights.shape[2]
    flat_weights = lax.optimization_barrier(weights.reshape(model_width, 2 * half_width))
    gathered = gather_tokens(tokens, flat_weights)
    projected = jnp.dot(gathered, flat_weights, preferred_element_type=jnp.float32)
    pre_grad, turned = local_backward(projected, out_grad)
    loss_scale = (gathered.shape[0] * 32) ** (-0.5)
    terms = Terms(flat_weights, model_width * 5 // 8)
    gradient_sum = sum_on_owners(pre_grad, turned, gathered, terms)
    new_master, new_first, new_second = adamw_update(
        gradient_sum * loss_scale, master, first_moment, second_moment
    )
    new_weights = gather_weights(new_master.astype(jnp.bfloat16), terms)
    input_grad = jnp.concatenate([terms.sum, terms.rest], axis=1)
    return (input_grad, new_weights, new_master, new_first, new_second)


def solution(mesh):
    dp, tensor = ("y_lo", "z", "core"), ("x", "y_hi")
    split = Mesh(mesh.devices.reshape(2, 8, 2, 4, 2), dp + tensor)
    owners = P(dp, None, tensor)
    return jax.shard_map(
        body,
        mesh=split,
        in_specs=(
            P(dp + tensor, None),
            P(dp, tensor),
            P(None, None, tensor),
            owners,
            owners,
            owners,
        ),
        out_specs=(P(dp + tensor, None), P(None, None, tensor), owners, owners, owners),
        check_vma=False,
    )
```

```python
import jax, jax.numpy as jnp
from jax import lax
from jax.experimental import pallas as pl
from jax.experimental.layout import Layout, with_layout_constraint
from jax.experimental.pallas import tpu as pltpu
from jax.sharding import Mesh, PartitionSpec as P

SEQ = 512
GROUP = 8

def scan_kernel(projected_ref, upstream_ref, out_ref, turned_ref, gate_ref, slope_ref):
    width = upstream_ref.shape[1]
    sequences = upstream_ref.shape[0] // SEQ
    row = lax.broadcasted_iota(jnp.int32, (GROUP, width), 0)
    zero = jnp.zeros((GROUP, width), jnp.float32)

    def down(x, k, fill):
        return jnp.where(row >= k, pltpu.roll(x, k, axis=0), fill)

    def up(x, k, fill):
        return jnp.where(row < GROUP - k, pltpu.roll(x, GROUP - k, axis=0), fill)

    def forward(step, carries):
        after = []
        for sequence in range(sequences):
            carry = carries[sequence]
            for half in range(2):
                rows = pl.ds(pl.multiple_of(sequence * SEQ + step * 16, 16) + half * 8, GROUP)
                gate = jax.nn.sigmoid(projected_ref[rows, :width])
                candidate = projected_ref[rows, width:]
                retain = 1.0 - gate
                factor, total = retain, gate * candidate
                for k in (1, 2, 4):
                    total = total + factor * down(total, k, 0.0)
                    factor = factor * down(factor, k, 1.0)
                hidden = total + factor * carry
                previous = jnp.where(row >= 1, pltpu.roll(hidden, 1, axis=0), carry)
                carry = jnp.broadcast_to(hidden[GROUP - 1 :], (GROUP, width))
                gate_ref[rows, :] = gate
                slope_ref[rows, :] = (candidate - previous) * gate * retain
            after.append(carry)
        return tuple(after)

    lax.fori_loop(0, SEQ // 16, forward, (zero,) * sequences, unroll=2)

    def backward(index, carries):
        step = SEQ // 16 - 1 - index
        after = []
        for sequence in range(sequences):
            carry = carries[sequence]
            base = pl.multiple_of(sequence * SEQ + step * 16, 16)
            upstream = upstream_ref[pl.ds(base, 16), :].astype(jnp.float32)
            halves = [None, None]
            for half in (1, 0):
                rows = pl.ds(base + half * 8, GROUP)
                incoming = upstream[half * 8 : half * 8 + 8]
                gate = gate_ref[rows, :]
                retain = 1.0 - gate
                factor, total = retain, retain * incoming
                for k in (1, 2, 4):
                    total = total + factor * up(total, k, 0.0)
                    factor = factor * up(factor, k, 1.0)
                passed = total + factor * carry
                adjoint = incoming + jnp.where(
                    row < GROUP - 1, pltpu.roll(passed, GROUP - 1, axis=0), carry
                )
                carry = jnp.broadcast_to(passed[:1], (GROUP, width))
                halves[half] = (adjoint * slope_ref[rows, :], adjoint * gate)
            after.append(carry)
            out_ref[pl.ds(base, 16), :width] = jnp.concatenate(
                [halves[0][0], halves[1][0]], axis=0
            ).astype(jnp.bfloat16)
            out_ref[pl.ds(base, 16), width:] = jnp.concatenate(
                [halves[0][1], halves[1][1]], axis=0
            ).astype(jnp.bfloat16)
        return tuple(after)

    lax.fori_loop(0, SEQ // 16, backward, (zero,) * sequences, unroll=2)
    turned_ref[...] = out_ref[...].T


def local_backward(projected, upstream):
    token_count, width = upstream.shape
    return pl.pallas_call(
        scan_kernel,
        out_shape=[
            jax.ShapeDtypeStruct((token_count, 2 * width), jnp.bfloat16),
            jax.ShapeDtypeStruct((2 * width, token_count), jnp.bfloat16),
        ],
        in_specs=[pl.BlockSpec(memory_space=pltpu.VMEM)] * 2,
        out_specs=[pl.BlockSpec(memory_space=pltpu.VMEM)] * 2,
        scratch_shapes=[
            pltpu.VMEM((token_count, width), jnp.float32),
            pltpu.VMEM((token_count, width), jnp.float32),
        ],
        compiler_params=pltpu.CompilerParams(vmem_limit_bytes=16 * 1024 * 1024),
        cost_estimate=pl.CostEstimate(
            flops=60 * token_count * width, bytes_accessed=14 * token_count * width,
            transcendentals=token_count * width,
        ),
    )(projected, upstream)


def adamw_update(gradient, master, first_moment, second_moment):
    new_first = 0.9 * first_moment + 0.1 * gradient
    new_second = 0.95 * second_moment + 0.05 * gradient * gradient
    update = new_first / (1.0 - 0.9**10) / (jnp.sqrt(new_second / (1.0 - 0.95**10)) + 1e-08)
    new_master = master - 0.001 * (update + 0.1 * master)
    return (new_master, new_first, new_second)


def shift(values, axis, step):
    size = lax.axis_size(axis)
    return lax.ppermute(values, axis, [(i, (i + step) % size) for i in range(size)])


def together(*values):
    return lax.optimization_barrier(values)


def gather_tokens(tokens, weights):
    rows, width = tokens.shape
    half = rows // 2
    at_x, at_y = lax.axis_index("x"), lax.axis_index("y_hi")
    cut = width // 2
    first, second = tokens[:, :cut], tokens[:, cut:]
    gathered = jnp.zeros((8 * rows, width), tokens.dtype)

    def put(gathered, block, dx, dy, row, column):
        owner = lax.rem(at_x + dx, 4) * 2 + lax.rem(at_y + dy, 2)
        return lax.dynamic_update_slice(gathered, block, (owner * rows + row, column))

    first_left, first_right = shift(first, "x", 1), shift(first, "x", 3)
    second_swap = shift(second, "y_hi", 1)
    (late,) = after(weights, first)
    first_swap = shift(late, "y_hi", 1)
    first_left, first_right, second_swap = together(first_left, first_right, second_swap)

    pair = jnp.concatenate([second, second_swap], axis=0)
    sides = jnp.concatenate([first_left, first_right], axis=0)
    far_top, far_bottom = shift(first_left[:half], "x", 1), shift(first_right[half:], "x", 3)
    pair_left, pair_right = shift(pair, "x", 1), shift(pair, "x", 3)
    sides_swap = shift(sides, "y_hi", 1)
    far_top, far_bottom, pair_left, pair_right = together(
        far_top, far_bottom, pair_left, pair_right
    )

    far = jnp.concatenate([far_top, far_bottom], axis=0)
    far_swap = shift(far, "y_hi", 1)
    pair_far_own, pair_far_other = shift(pair_left[:rows], "x", 1), shift(pair_right[rows:], "x", 3)

    gathered = put(gathered, tokens, 0, 0, 0, 0)
    gathered = put(gathered, first_left, 3, 0, 0, 0)
    gathered = put(gathered, first_right, 1, 0, 0, 0)
    gathered = put(gathered, second_swap, 0, 1, 0, cut)
    gathered = put(gathered, first_swap, 0, 1, 0, 0)
    gathered = put(gathered, far, 2, 0, 0, 0)
    for block, dx in ((pair_left, 3), (pair_right, 1)):
        gathered = put(gathered, block[:rows], dx, 0, 0, cut)
        gathered = put(gathered, block[rows:], dx, 1, 0, cut)
    gathered = put(gathered, sides_swap[:rows], 3, 1, 0, 0)
    gathered = put(gathered, sides_swap[rows:], 1, 1, 0, 0)
    gathered = put(gathered, far_swap, 2, 1, 0, 0)
    gathered = put(gathered, pair_far_own, 2, 0, 0, cut)
    gathered = put(gathered, pair_far_other, 2, 1, 0, cut)
    return gathered


def around(values):
    up = [(2 * i, 2 * ((i + 1) % 8)) for i in range(8)]
    down = [(2 * i + 1, 2 * ((i + 7) % 8) + 1) for i in range(8)]
    return lax.ppermute(values, ("z", "core"), up + down)


def add(*values):
    total = values[0].astype(jnp.float32)
    for value in values[1:]:
        total = total + value.astype(jnp.float32)
    return total.astype(jnp.bfloat16)


def products_kernel(order_ref, turned_ref, tokens_ref, *out_refs):
    step = pl.program_id(0)
    value = jnp.dot(
        turned_ref[...], tokens_ref[...], preferred_element_type=jnp.float32
    ).astype(out_refs[0].dtype)
    for out_ref, first, last in zip(out_refs, (0, 2, 8), (2, 8, 16)):

        @pl.when((step >= first) & (step < last))
        def _(out_ref=out_ref):
            out_ref[0] = value


def products(turned, gathered, order):
    width, token_count = turned.shape
    rows = gathered.shape[1] // 16
    block = (1, width, rows)
    return pl.pallas_call(
        products_kernel,
        out_shape=[
            jax.ShapeDtypeStruct((count, width, rows), jnp.bfloat16) for count in (2, 6, 8)
        ],
        grid_spec=pltpu.PrefetchScalarGridSpec(
            num_scalar_prefetch=1,
            grid=(16,),
            in_specs=[
                pl.BlockSpec((width, token_count), lambda step, order: (0, 0)),
                pl.BlockSpec((token_count, rows), lambda step, order: (0, order[step])),
            ],
            out_specs=[
                pl.BlockSpec(block, lambda step, order: (jnp.minimum(step, 1), 0, 0)),
                pl.BlockSpec(block, lambda step, order: (jnp.clip(step - 2, 0, 5), 0, 0)),
                pl.BlockSpec(block, lambda step, order: (jnp.maximum(step - 8, 0), 0, 0)),
            ],
        ),
        compiler_params=pltpu.CompilerParams(vmem_limit_bytes=10 * 1024 * 1024),
        cost_estimate=pl.CostEstimate(
            flops=32 * width * rows * token_count,
            bytes_accessed=2 * (token_count * (width + 16 * rows) + 16 * width * rows),
            transcendentals=0,
        ),
    )(jnp.stack(order).astype(jnp.int32), turned, gathered)


def after(token, *values):
    return together(token, *values)[1:]


def sum_on_owners(pre_grad, turned, gathered, terms):
    at_core, at_z, at_y = (lax.axis_index(name) for name in ("core", "z", "y_lo"))
    sign = 1 - 2 * at_core
    rows = gathered.shape[1] // 16
    rings = [1 - at_y, at_y]

    def place(distance, y):
        return y * 8 + lax.rem(at_z + distance + 8, 8)

    def columns(total):
        own = lax.dynamic_slice_in_dim(total, at_core * (rows // 2), rows // 2, axis=1)
        other = lax.dynamic_slice_in_dim(total, (1 - at_core) * (rows // 2), rows // 2, axis=1)
        return own, other

    order = [place(4, 1 - at_core), place(4, at_core)]
    order += [place(-sign * distance, y) for distance in (3, 2, 1) for y in rings]
    order += [place(sign * distance, y) for distance in (3, 2, 1, 0) for y in rings]
    far, sent, kept = products(turned, gathered, order)
    crossed_far = shift(far[0], "core", 1)
    crossed = shift(sent, "core", 1)
    (late,) = after(kept, pre_grad)
    offloaded = terms.start(late)
    (near,) = after(offloaded, far[1])
    far = around(add(near, crossed_far))
    none = jnp.zeros((), far.dtype)
    running = [jnp.where(y == at_core, far, none) for y in rings]
    for step in range(3):
        for ring in range(2):
            position = 2 * step + ring
            value = add(kept[position], crossed[position], running[ring])
            running[ring] = around(value)
        if step == 0:
            terms.first(value)
    (near, _, _) = together(kept[6], *terms.second(value))
    straight, diagonal = columns(add(near, running[0]))
    straight = shift(straight, "y_lo", 1)
    diagonal = lax.ppermute(diagonal, ("y_lo", "core"), [(i, 3 - i) for i in range(4)])
    own, crossed = columns(add(kept[7], running[1]))
    crossed = shift(crossed, "core", 1)
    total = sum(value.astype(jnp.float32) for value in (own, crossed, straight, diagonal))
    return total.T.reshape(rows // 2, 2, -1)


def row_major(values):
    return with_layout_constraint(values, Layout(major_to_minor=tuple(range(values.ndim))))


def place_kernel(block_ref, out_ref, semaphore):
    at_y, at_z = lax.axis_index("y_lo"), lax.axis_index("z")
    copy = pltpu.make_async_copy(block_ref, out_ref.at[at_y, at_z], semaphore)
    copy.start()
    copy.wait()


def place(block):
    return pl.pallas_call(
        place_kernel,
        out_shape=jax.ShapeDtypeStruct((2, 8) + block.shape, block.dtype),
        in_specs=[pl.BlockSpec(memory_space=pltpu.VMEM)],
        out_specs=pl.BlockSpec(memory_space=pl.ANY),
        scratch_shapes=[pltpu.SemaphoreType.DMA],
        cost_estimate=pl.CostEstimate(flops=0, bytes_accessed=4 * block.size, transcendentals=0),
    )(block)


def gather_weights(owned, terms):
    at_core, at_z, at_y = (lax.axis_index(name) for name in ("core", "z", "y_lo"))
    sign = 1 - 2 * at_core
    rows = owned.shape[0]
    rings = [at_y, 1 - at_y]

    def put(result, block, distance, y, row=0):
        return lax.dynamic_update_slice(
            result, block[None, None], (y, lax.rem(at_z + distance + 8, 8), row, 0, 0)
        )

    def swap(values, axis):
        return row_major(shift(values, axis, 1))

    def by_core(mine, others):
        return row_major(
            jnp.where(
                at_core == 0,
                jnp.concatenate([mine, others], axis=0),
                jnp.concatenate([others, mine], axis=0),
            )
        )

    owned = row_major(owned)
    across = swap(owned, "y_lo")
    moving = [by_core(owned, swap(owned, "core"))]
    received = [row_major(around(moving[0]))]
    (across,) = after(moving[0], across)
    moving.append(by_core(across, swap(across, "core")))
    received.append(row_major(around(moving[1])))
    terms.third(moving[1])
    result = put(place(moving[0]), moving[1], 0, rings[1])
    for step in (1, 2, 3):
        for ring, y in enumerate(rings):
            moving = received[ring]
            if step < 3:
                received[ring] = row_major(around(moving))
            else:
                sent = lax.dynamic_slice_in_dim(moving, at_core * rows, rows, axis=0)
                received[ring] = row_major(around(row_major(sent)))
            crossed = swap(moving, "core")
            result = put(result, moving, -sign * step, y)
            result = put(result, crossed, sign * step, y)
            result, received[ring] = together(result, received[ring])
    result, terms.whole = together(result, terms.last(received[0]))
    for ring, y in enumerate(rings):
        crossed = swap(received[ring], "core")
        result = put(result, received[ring], 4, y, at_core * rows)
        result = put(result, crossed, 4, y, (1 - at_core) * rows)
    return result.reshape((32 * rows,) + owned.shape[1:])


def terms_kernel(pre_ref, weights_ref, out_ref):
    out_ref[...] = lax.dot_general(
        pre_ref[...],
        weights_ref[...],
        (((1,), (1,)), ((), ())),
        preferred_element_type=jnp.float32,
    ).astype(out_ref.dtype)


def all_terms(pre_grad, weights, columns):
    token_count, width = pre_grad.shape
    block = 512
    return pl.pallas_call(
        terms_kernel,
        out_shape=jax.ShapeDtypeStruct((token_count, columns), pre_grad.dtype),
        grid=(columns // block,),
        in_specs=[
            pl.BlockSpec((token_count, width), lambda step: (0, 0)),
            pl.BlockSpec((block, width), lambda step: (step, 0)),
        ],
        out_specs=pl.BlockSpec((token_count, block), lambda step: (0, step)),
        compiler_params=pltpu.CompilerParams(vmem_limit_bytes=12 * 1024 * 1024),
        cost_estimate=pl.CostEstimate(
            flops=2 * token_count * width * columns,
            bytes_accessed=2 * (token_count * width + columns * (width + token_count)),
            transcendentals=0,
        ),
    )(pre_grad, weights)


class Terms:
    def __init__(self, weights, offloaded):
        self.weights = weights
        self.offloaded = offloaded

    def dot(self, values, weights):
        return lax.dot_general(
            values, weights, (((1,), (1,)), ((), ())), preferred_element_type=jnp.float32
        ).astype(jnp.bfloat16)

    def part(self, distance):
        rows = self.pre_grad.shape[0] // 4
        start = lax.rem(lax.axis_index("x") + distance, 4) * rows
        values = lax.dynamic_slice_in_dim(self.pre_grad, start, rows, axis=0)
        return self.dot(values, self.weights[self.offloaded :])

    def start(self, pre_grad):
        self.pre_grad = pre_grad
        self.rows = pre_grad.shape[0] // 8
        offloaded = all_terms(pre_grad, self.weights, self.offloaded)
        self.sum = lax.psum_scatter(offloaded, ("x", "y_hi"), scatter_dimension=0, tiled=True)
        return offloaded

    def first(self, token):
        (self.pre_grad,) = after(token, self.pre_grad)
        far = self.part(2)
        self.moved = shift(far[: self.rows], "x", 1), shift(far[self.rows :], "x", 3)
        return far

    def second(self, token):
        from_left, from_right = after(token, *self.moved)
        rows = self.rows
        right, left = self.part(1), self.part(3)
        right = jnp.concatenate([add(right[:rows], from_left), right[rows:]], axis=0)
        left = jnp.concatenate([left[:rows], add(left[rows:], from_right)], axis=0)
        self.moved = shift(right, "x", 1), shift(left, "x", 3)
        return right, left

    def third(self, token):
        from_left, from_right = after(token, *self.moved)
        at_y = lax.axis_index("y_hi")
        total = add(self.part(0), from_left, from_right).reshape(2, self.rows, -1)
        self.own = lax.dynamic_index_in_dim(total, at_y, 0, keepdims=False)
        other = lax.dynamic_index_in_dim(total, 1 - at_y, 0, keepdims=False)
        self.moved = shift(other, "y_hi", 1)

    def last(self, token):
        (moved,) = after(token, self.moved)
        return jnp.concatenate([self.sum, add(self.own, moved)], axis=1)


def body(tokens, out_grad, weights, master, first_moment, second_moment):
    model_width = weights.shape[0]
    half_width = weights.shape[2]
    flat_weights = lax.optimization_barrier(weights.reshape(model_width, 2 * half_width))
    gathered = gather_tokens(tokens, flat_weights)
    projected = jnp.dot(gathered, flat_weights, preferred_element_type=jnp.float32)
    pre_grad, turned = local_backward(projected, out_grad)
    loss_scale = (gathered.shape[0] * 32) ** (-0.5)
    terms = Terms(flat_weights, model_width * 3 // 4)
    gradient_sum = sum_on_owners(pre_grad, turned, gathered, terms)
    new_master, new_first, new_second = adamw_update(
        gradient_sum * loss_scale, master, first_moment, second_moment
    )
    new_weights = gather_weights(new_master.astype(jnp.bfloat16), terms)
    return (terms.whole, new_weights, new_master, new_first, new_second)


def solution(mesh):
    dp, tensor = ("y_lo", "z", "core"), ("x", "y_hi")
    split = Mesh(mesh.devices.reshape(2, 8, 2, 4, 2), dp + tensor)
    owners = P(dp, None, tensor)
    return jax.shard_map(
        body,
        mesh=split,
        in_specs=(
            P(dp + tensor, None),
            P(dp, tensor),
            P(None, None, tensor),
            owners,
            owners,
            owners,
        ),
        out_specs=(P(dp + tensor, None), P(None, None, tensor), owners, owners, owners),
        check_vma=False,
    )
```

```python
import jax, jax.numpy as jnp
from jax import lax
from jax.experimental import pallas as pl
from jax.experimental.layout import Layout, with_layout_constraint
from jax.experimental.pallas import tpu as pltpu
from jax.sharding import Mesh, PartitionSpec as P

SEQ = 512
GROUP = 8

def scan_kernel(projected_ref, upstream_ref, out_ref, turned_ref, gate_ref, slope_ref):
    width = upstream_ref.shape[1]
    sequences = upstream_ref.shape[0] // SEQ
    row = lax.broadcasted_iota(jnp.int32, (GROUP, width), 0)
    zero = jnp.zeros((GROUP, width), jnp.float32)

    def down(x, k, fill):
        return jnp.where(row >= k, pltpu.roll(x, k, axis=0), fill)

    def up(x, k, fill):
        return jnp.where(row < GROUP - k, pltpu.roll(x, GROUP - k, axis=0), fill)

    def forward(step, carries):
        after = []
        for sequence in range(sequences):
            carry = carries[sequence]
            for half in range(2):
                rows = pl.ds(pl.multiple_of(sequence * SEQ + step * 16, 16) + half * 8, GROUP)
                gate = jax.nn.sigmoid(projected_ref[rows, :width])
                candidate = projected_ref[rows, width:]
                retain = 1.0 - gate
                factor, total = retain, gate * candidate
                for k in (1, 2, 4):
                    total = total + factor * down(total, k, 0.0)
                    factor = factor * down(factor, k, 1.0)
                hidden = total + factor * carry
                previous = jnp.where(row >= 1, pltpu.roll(hidden, 1, axis=0), carry)
                carry = jnp.broadcast_to(hidden[GROUP - 1 :], (GROUP, width))
                gate_ref[rows, :] = gate
                slope_ref[rows, :] = (candidate - previous) * gate * retain
            after.append(carry)
        return tuple(after)

    lax.fori_loop(0, SEQ // 16, forward, (zero,) * sequences, unroll=2)

    def backward(index, carries):
        step = SEQ // 16 - 1 - index
        after = []
        for sequence in range(sequences):
            carry = carries[sequence]
            base = pl.multiple_of(sequence * SEQ + step * 16, 16)
            upstream = upstream_ref[pl.ds(base, 16), :].astype(jnp.float32)
            halves = [None, None]
            for half in (1, 0):
                rows = pl.ds(base + half * 8, GROUP)
                incoming = upstream[half * 8 : half * 8 + 8]
                gate = gate_ref[rows, :]
                retain = 1.0 - gate
                factor, total = retain, retain * incoming
                for k in (1, 2, 4):
                    total = total + factor * up(total, k, 0.0)
                    factor = factor * up(factor, k, 1.0)
                passed = total + factor * carry
                adjoint = incoming + jnp.where(
                    row < GROUP - 1, pltpu.roll(passed, GROUP - 1, axis=0), carry
                )
                carry = jnp.broadcast_to(passed[:1], (GROUP, width))
                halves[half] = (adjoint * slope_ref[rows, :], adjoint * gate)
            after.append(carry)
            out_ref[pl.ds(base, 16), :width] = jnp.concatenate(
                [halves[0][0], halves[1][0]], axis=0
            ).astype(jnp.bfloat16)
            out_ref[pl.ds(base, 16), width:] = jnp.concatenate(
                [halves[0][1], halves[1][1]], axis=0
            ).astype(jnp.bfloat16)
        return tuple(after)

    lax.fori_loop(0, SEQ // 16, backward, (zero,) * sequences, unroll=2)
    turned_ref[...] = out_ref[...].T


def local_backward(projected, upstream):
    token_count, width = upstream.shape
    return pl.pallas_call(
        scan_kernel,
        out_shape=[
            jax.ShapeDtypeStruct((token_count, 2 * width), jnp.bfloat16),
            jax.ShapeDtypeStruct((2 * width, token_count), jnp.bfloat16),
        ],
        in_specs=[pl.BlockSpec(memory_space=pltpu.VMEM)] * 2,
        out_specs=[pl.BlockSpec(memory_space=pltpu.VMEM)] * 2,
        scratch_shapes=[
            pltpu.VMEM((token_count, width), jnp.float32),
            pltpu.VMEM((token_count, width), jnp.float32),
        ],
        compiler_params=pltpu.CompilerParams(vmem_limit_bytes=16 * 1024 * 1024),
        cost_estimate=pl.CostEstimate(
            flops=60 * token_count * width, bytes_accessed=14 * token_count * width,
            transcendentals=token_count * width,
        ),
    )(projected, upstream)


def adamw_update(gradient, master, first_moment, second_moment):
    new_first = 0.9 * first_moment + 0.1 * gradient
    new_second = 0.95 * second_moment + 0.05 * gradient * gradient
    update = new_first / (1.0 - 0.9**10) / (jnp.sqrt(new_second / (1.0 - 0.95**10)) + 1e-08)
    new_master = master - 0.001 * (update + 0.1 * master)
    return (new_master, new_first, new_second)


def shift(values, axis, step):
    size = lax.axis_size(axis)
    return lax.ppermute(values, axis, [(i, (i + step) % size) for i in range(size)])


def together(*values):
    return lax.optimization_barrier(values)


def gather_tokens(tokens, weights):
    rows, width = tokens.shape
    half = rows // 2
    at_x, at_y = lax.axis_index("x"), lax.axis_index("y_hi")
    cut = width // 2
    first, second = tokens[:, :cut], tokens[:, cut:]
    gathered = jnp.zeros((8 * rows, width), tokens.dtype)

    def put(gathered, block, dx, dy, row, column):
        owner = lax.rem(at_x + dx, 4) * 2 + lax.rem(at_y + dy, 2)
        return lax.dynamic_update_slice(gathered, block, (owner * rows + row, column))

    first_left, first_right = shift(first, "x", 1), shift(first, "x", 3)
    second_swap = shift(second, "y_hi", 1)
    (late,) = after(weights, first)
    first_swap = shift(late, "y_hi", 1)
    first_left, first_right, second_swap = together(first_left, first_right, second_swap)

    pair = jnp.concatenate([second, second_swap], axis=0)
    sides = jnp.concatenate([first_left, first_right], axis=0)
    far_top, far_bottom = shift(first_left[:half], "x", 1), shift(first_right[half:], "x", 3)
    pair_left, pair_right = shift(pair, "x", 1), shift(pair, "x", 3)
    sides_swap = shift(sides, "y_hi", 1)
    far_top, far_bottom, pair_left, pair_right = together(
        far_top, far_bottom, pair_left, pair_right
    )

    far = jnp.concatenate([far_top, far_bottom], axis=0)
    far_swap = shift(far, "y_hi", 1)
    pair_far_own, pair_far_other = shift(pair_left[:rows], "x", 1), shift(pair_right[rows:], "x", 3)

    gathered = put(gathered, tokens, 0, 0, 0, 0)
    gathered = put(gathered, first_left, 3, 0, 0, 0)
    gathered = put(gathered, first_right, 1, 0, 0, 0)
    gathered = put(gathered, second_swap, 0, 1, 0, cut)
    gathered = put(gathered, first_swap, 0, 1, 0, 0)
    gathered = put(gathered, far, 2, 0, 0, 0)
    for block, dx in ((pair_left, 3), (pair_right, 1)):
        gathered = put(gathered, block[:rows], dx, 0, 0, cut)
        gathered = put(gathered, block[rows:], dx, 1, 0, cut)
    gathered = put(gathered, sides_swap[:rows], 3, 1, 0, 0)
    gathered = put(gathered, sides_swap[rows:], 1, 1, 0, 0)
    gathered = put(gathered, far_swap, 2, 1, 0, 0)
    gathered = put(gathered, pair_far_own, 2, 0, 0, cut)
    gathered = put(gathered, pair_far_other, 2, 1, 0, cut)
    return gathered


def around(values):
    up = [(2 * i, 2 * ((i + 1) % 8)) for i in range(8)]
    down = [(2 * i + 1, 2 * ((i + 7) % 8) + 1) for i in range(8)]
    return lax.ppermute(values, ("z", "core"), up + down)


def add(*values):
    total = values[0].astype(jnp.float32)
    for value in values[1:]:
        total = total + value.astype(jnp.float32)
    return total.astype(jnp.bfloat16)


def products_kernel(order_ref, turned_ref, tokens_ref, *out_refs):
    rows = out_refs[0].shape[2]
    first = 0
    for out_ref in out_refs:

        def one(index, carry, out_ref=out_ref, first=first):
            start = pl.multiple_of(order_ref[first + index] * rows, rows)
            out_ref[index] = jnp.dot(
                turned_ref[...],
                tokens_ref[:, pl.ds(start, rows)],
                preferred_element_type=jnp.float32,
            ).astype(out_ref.dtype)
            return carry

        lax.fori_loop(0, out_ref.shape[0], one, 0)
        first += out_ref.shape[0]


def products(turned, gathered, order):
    width, token_count = turned.shape
    rows = gathered.shape[1] // 16
    return pl.pallas_call(
        products_kernel,
        out_shape=[
            jax.ShapeDtypeStruct((count, width, rows), jnp.bfloat16) for count in (2, 6, 8)
        ],
        in_specs=[
            pl.BlockSpec(memory_space=pltpu.SMEM),
            pl.BlockSpec(memory_space=pltpu.VMEM),
            pl.BlockSpec(memory_space=pltpu.VMEM),
        ],
        out_specs=[pl.BlockSpec(memory_space=pltpu.VMEM)] * 3,
        compiler_params=pltpu.CompilerParams(vmem_limit_bytes=24 * 1024 * 1024),
        cost_estimate=pl.CostEstimate(
            flops=32 * width * rows * token_count,
            bytes_accessed=2 * (token_count * (width + 16 * rows) + 16 * width * rows),
            transcendentals=0,
        ),
    )(jnp.stack(order).astype(jnp.int32), turned, gathered)


def after(token, *values):
    return together(token, *values)[1:]


def sum_on_owners(pre_grad, turned, gathered, terms):
    at_core, at_z, at_y = (lax.axis_index(name) for name in ("core", "z", "y_lo"))
    sign = 1 - 2 * at_core
    rows = gathered.shape[1] // 16
    rings = [1 - at_y, at_y]

    def place(distance, y):
        return y * 8 + lax.rem(at_z + distance + 8, 8)

    def columns(total):
        own = lax.dynamic_slice_in_dim(total, at_core * (rows // 2), rows // 2, axis=1)
        other = lax.dynamic_slice_in_dim(total, (1 - at_core) * (rows // 2), rows // 2, axis=1)
        return own, other

    order = [place(4, 1 - at_core), place(4, at_core)]
    order += [place(-sign * distance, y) for distance in (3, 2, 1) for y in rings]
    order += [place(sign * distance, y) for distance in (3, 2, 1, 0) for y in rings]
    far, sent, kept = products(turned, gathered, order)
    crossed_far = shift(far[0], "core", 1)
    crossed = shift(sent, "core", 1)
    (late,) = after(kept, pre_grad)
    offloaded = terms.start(late)
    (near,) = after(offloaded, far[1])
    far = around(add(near, crossed_far))
    none = jnp.zeros((), far.dtype)
    running = [jnp.where(y == at_core, far, none) for y in rings]
    for step in range(3):
        for ring in range(2):
            position = 2 * step + ring
            value = add(kept[position], crossed[position], running[ring])
            running[ring] = around(value)
        if step == 0:
            terms.first(value)
    (near, _, _) = together(kept[6], *terms.second(value))
    straight, diagonal = columns(add(near, running[0]))
    straight = shift(straight, "y_lo", 1)
    diagonal = lax.ppermute(diagonal, ("y_lo", "core"), [(i, 3 - i) for i in range(4)])
    own, crossed = columns(add(kept[7], running[1]))
    crossed = shift(crossed, "core", 1)
    total = sum(value.astype(jnp.float32) for value in (own, crossed, straight, diagonal))
    return total.T.reshape(rows // 2, 2, -1)


def row_major(values):
    return with_layout_constraint(values, Layout(major_to_minor=tuple(range(values.ndim))))


def place_kernel(block_ref, out_ref, semaphore):
    at_y, at_z = lax.axis_index("y_lo"), lax.axis_index("z")
    copy = pltpu.make_async_copy(block_ref, out_ref.at[at_y, at_z], semaphore)
    copy.start()
    copy.wait()


def place(block):
    return pl.pallas_call(
        place_kernel,
        out_shape=jax.ShapeDtypeStruct((2, 8) + block.shape, block.dtype),
        in_specs=[pl.BlockSpec(memory_space=pltpu.VMEM)],
        out_specs=pl.BlockSpec(memory_space=pl.ANY),
        scratch_shapes=[pltpu.SemaphoreType.DMA],
        cost_estimate=pl.CostEstimate(flops=0, bytes_accessed=4 * block.size, transcendentals=0),
    )(block)


def gather_weights(owned, terms):
    at_core, at_z, at_y = (lax.axis_index(name) for name in ("core", "z", "y_lo"))
    sign = 1 - 2 * at_core
    rows = owned.shape[0]
    rings = [at_y, 1 - at_y]

    def put(result, block, distance, y, row=0):
        return lax.dynamic_update_slice(
            result, block[None, None], (y, lax.rem(at_z + distance + 8, 8), row, 0, 0)
        )

    def swap(values, axis):
        return row_major(shift(values, axis, 1))

    def by_core(mine, others):
        return row_major(
            jnp.where(
                at_core == 0,
                jnp.concatenate([mine, others], axis=0),
                jnp.concatenate([others, mine], axis=0),
            )
        )

    owned = row_major(owned)
    across = swap(owned, "y_lo")
    moving = [by_core(owned, swap(owned, "core"))]
    received = [row_major(around(moving[0]))]
    (across,) = after(moving[0], across)
    moving.append(by_core(across, swap(across, "core")))
    received.append(row_major(around(moving[1])))
    terms.third(moving[1])
    result = put(place(moving[0]), moving[1], 0, rings[1])
    for step in (1, 2, 3):
        for ring, y in enumerate(rings):
            moving = received[ring]
            if step < 3:
                received[ring] = row_major(around(moving))
            else:
                sent = lax.dynamic_slice_in_dim(moving, at_core * rows, rows, axis=0)
                received[ring] = row_major(around(row_major(sent)))
            crossed = swap(moving, "core")
            result = put(result, moving, -sign * step, y)
            result = put(result, crossed, sign * step, y)
            result, received[ring] = together(result, received[ring])
    result, terms.whole = together(result, terms.last(received[0]))
    for ring, y in enumerate(rings):
        crossed = swap(received[ring], "core")
        result = put(result, received[ring], 4, y, at_core * rows)
        result = put(result, crossed, 4, y, (1 - at_core) * rows)
    return result.reshape((32 * rows,) + owned.shape[1:])


def terms_kernel(pre_ref, weights_ref, out_ref):
    out_ref[...] = lax.dot_general(
        pre_ref[...],
        weights_ref[...],
        (((1,), (1,)), ((), ())),
        preferred_element_type=jnp.float32,
    ).astype(out_ref.dtype)


def all_terms(pre_grad, weights, columns):
    token_count, width = pre_grad.shape
    block = 512
    return pl.pallas_call(
        terms_kernel,
        out_shape=jax.ShapeDtypeStruct((token_count, columns), pre_grad.dtype),
        grid=(columns // block,),
        in_specs=[
            pl.BlockSpec((token_count, width), lambda step: (0, 0)),
            pl.BlockSpec((block, width), lambda step: (step, 0)),
        ],
        out_specs=pl.BlockSpec((token_count, block), lambda step: (0, step)),
        compiler_params=pltpu.CompilerParams(vmem_limit_bytes=12 * 1024 * 1024),
        cost_estimate=pl.CostEstimate(
            flops=2 * token_count * width * columns,
            bytes_accessed=2 * (token_count * width + columns * (width + token_count)),
            transcendentals=0,
        ),
    )(pre_grad, weights)


class Terms:
    def __init__(self, weights, offloaded):
        self.weights = weights
        self.offloaded = offloaded

    def dot(self, values, weights):
        return lax.dot_general(
            values, weights, (((1,), (1,)), ((), ())), preferred_element_type=jnp.float32
        ).astype(jnp.bfloat16)

    def part(self, distance):
        rows = self.pre_grad.shape[0] // 4
        start = lax.rem(lax.axis_index("x") + distance, 4) * rows
        values = lax.dynamic_slice_in_dim(self.pre_grad, start, rows, axis=0)
        return self.dot(values, self.weights[self.offloaded :])

    def start(self, pre_grad):
        self.pre_grad = pre_grad
        self.rows = pre_grad.shape[0] // 8
        offloaded = all_terms(pre_grad, self.weights, self.offloaded)
        self.sum = lax.psum_scatter(offloaded, ("x", "y_hi"), scatter_dimension=0, tiled=True)
        return offloaded

    def first(self, token):
        (self.pre_grad,) = after(token, self.pre_grad)
        far = self.part(2)
        self.moved = shift(far[: self.rows], "x", 1), shift(far[self.rows :], "x", 3)
        return far

    def second(self, token):
        from_left, from_right = after(token, *self.moved)
        rows = self.rows
        right, left = self.part(1), self.part(3)
        right = jnp.concatenate([add(right[:rows], from_left), right[rows:]], axis=0)
        left = jnp.concatenate([left[:rows], add(left[rows:], from_right)], axis=0)
        self.moved = shift(right, "x", 1), shift(left, "x", 3)
        return right, left

    def third(self, token):
        from_left, from_right = after(token, *self.moved)
        at_y = lax.axis_index("y_hi")
        total = add(self.part(0), from_left, from_right).reshape(2, self.rows, -1)
        self.own = lax.dynamic_index_in_dim(total, at_y, 0, keepdims=False)
        other = lax.dynamic_index_in_dim(total, 1 - at_y, 0, keepdims=False)
        self.moved = shift(other, "y_hi", 1)

    def last(self, token):
        (moved,) = after(token, self.moved)
        return jnp.concatenate([self.sum, add(self.own, moved)], axis=1)


def body(tokens, out_grad, weights, master, first_moment, second_moment):
    model_width = weights.shape[0]
    half_width = weights.shape[2]
    flat_weights = lax.optimization_barrier(weights.reshape(model_width, 2 * half_width))
    gathered = gather_tokens(tokens, flat_weights)
    projected = jnp.dot(gathered, flat_weights, preferred_element_type=jnp.float32)
    pre_grad, turned = local_backward(projected, out_grad)
    loss_scale = (gathered.shape[0] * 32) ** (-0.5)
    terms = Terms(flat_weights, model_width * 3 // 4)
    gradient_sum = sum_on_owners(pre_grad, turned, gathered, terms)
    new_master, new_first, new_second = adamw_update(
        gradient_sum * loss_scale, master, first_moment, second_moment
    )
    new_weights = gather_weights(new_master.astype(jnp.bfloat16), terms)
    return (terms.whole, new_weights, new_master, new_first, new_second)


def solution(mesh):
    dp, tensor = ("y_lo", "z", "core"), ("x", "y_hi")
    split = Mesh(mesh.devices.reshape(2, 8, 2, 4, 2), dp + tensor)
    owners = P(dp, None, tensor)
    return jax.shard_map(
        body,
        mesh=split,
        in_specs=(
            P(dp + tensor, None),
            P(dp, tensor),
            P(None, None, tensor),
            owners,
            owners,
            owners,
        ),
        out_specs=(P(dp + tensor, None), P(None, None, tensor), owners, owners, owners),
        check_vma=False,
    )
```
